32 devices in a mesh: fld: 4 (over z), wn: 8 (over y, x, core).
Axes of the slice: x: 2, y: 2, z: 4, core: 2. Of those that a mesh axis runs over, the one named last changes fastest.
Arguments:
- spec_tq: bfloat16 [640, 2, 16, 2, 1281], P('wn', None, 'fld'), may hold values from -0.119628906 to 0.119628906
- spec_sp: bfloat16 [640, 2, 1281], P('wn'), may hold values from -0.119628906 to 0.119628906
- legendre: bfloat16 [640, 128, 1281], P('wn'), may hold values from -0.15625 to 0.15625
- low_wavenumber: int32 [640], replicated, may hold values from 0 to 639, each once
- lon_points: int32 [128], replicated, may hold values from 20 to 5136, as said below
- requested_elevation: int32 [256, 5632], P('wn', 'fld'), may hold values from 30 to 1599
Outputs:
- temperature_anomaly: float32 [256, 5632], P('wn', 'fld')
- humidity_ratio: float32 [256, 5632], P('wn', 'fld')
The draws below stay inside these ranges and needn't reach their ends.
Inputs may be any that keep to these rules, and one draw needn't show every extreme that they name: `low_wavenumber`: every number 0 to 639 is the lower wavenumber of exactly one pair. `lon_points`: row entries are 4 j + 16 for octahedral row numbers j between 1 and 1280, not decreasing along the rows; the first row has 20 points and the last row 5136.
All inputs are finite; a program needn't handle non-finite values.
Results may differ from the reference program's by a relative error of at most 0.0037.
Values sent between devices are 32-bit elements; how exact they have to be, the bound alone decides.
No kernel may reach another device: no remote copies, remote signals or barrier semaphores. Data moves between devices by JAX's collectives and lax.ppermute only.
A program may use at most 192 MiB of HBM per device.

```python
import math
import jax
import jax.numpy as jnp
from jax import lax

MW = 1280
STRATUM_COUNT = 16
PAIRS = 640
K = 1281
LONPAD = 5632
LAT = 256
LATH = 128


def draw_lon_points(key, part):
    row_numbers = jax.random.randint(key, (LATH,), 1, MW + 1)
    row_numbers = jnp.sort(row_numbers)
    final_row = jnp.arange(LATH) == LATH - 1
    first_row = jnp.arange(LATH) == 0
    row_numbers = jnp.where(final_row, MW, row_numbers)
    row_numbers = jnp.where(first_row, 1, row_numbers)
    return (4 * row_numbers + 16).astype(jnp.int32)


def place_ends(entries, stream_key, low, high):
    index_at = [jax.random.randint(jax.random.fold_in(stream_key, axis), (), 0, length) for axis, length in enumerate(entries.shape)]
    longest = entries.shape.index(max(entries.shape))
    next_to = index_at[:longest] + [(index_at[longest] + 1) % entries.shape[longest]] + index_at[longest + 1:]
    return entries.at[tuple(index_at)].set(low).at[tuple(next_to)].set(high)


def level_of(stream_key, extent, shards, least, high):
    loudness, own = 1.0, jax.random.fold_in(stream_key, 6)
    for dim, shards_of in shards:
        heights = jnp.exp(jax.random.uniform(jax.random.fold_in(own, dim), (shards_of,), jnp.float32, least / len(shards), high / len(shards)))
        loudness = loudness * jnp.repeat(heights, extent[dim] // shards_of).reshape([-1 if axis == dim else 1 for axis in range(len(extent))])
    return loudness


def noise(key, extent, spread, most, cuts=(), kind=jnp.bfloat16):
    values = jax.random.normal(key, extent, jnp.float32) * spread
    if len(cuts) > 0:
        values = level_of(key, extent, cuts, -0.22, 0.18) * values
    return jnp.clip(values, min=-most, max=most).astype(kind)


def setup_inputs(seed: int = 0) -> dict:
    arg_keys = jax.random.split(jax.random.key(seed), 7)
    return {
        "spec_tq": noise(arg_keys[0], (PAIRS, 2, STRATUM_COUNT, 2, K), 0.02, 0.119628906, ((0, 8), (2, 4))),
        "spec_sp": noise(arg_keys[1], (PAIRS, 2, K), 0.02, 0.119628906, ((0, 8),)),
        "legendre": noise(arg_keys[2], (PAIRS, LATH, K), K ** -0.5, 0.15625, ((0, 8),)),
        "low_wavenumber": jax.random.permutation(arg_keys[3], PAIRS).astype(jnp.int32),
        "lon_points": draw_lon_points(jax.random.fold_in(arg_keys[6], 71), 0),
        "requested_elevation": place_ends(jax.random.randint(arg_keys[5], (LAT, LONPAD), 30, 100 * STRATUM_COUNT), jax.random.fold_in(arg_keys[5], 1), 30, (100 * STRATUM_COUNT) - 1).astype(jnp.int32),
    }


group_width = 128
thickness_scale = 0.012 * 287.05 / 9.80665
log_step = 0.012


def wave_table(wave_line, points, group_ids):
    residue = (wave_line[:, None] * (group_ids[None, :] * group_width)) % points
    phase = residue.astype(jnp.float32) * (2.0 * math.pi / points.astype(jnp.float32))
    return jnp.concatenate([jnp.cos(phase), -jnp.sin(phase)], 0).astype(jnp.bfloat16)


def twisted(coeffs, wave_line, points):
    lanes = jnp.arange(group_width, dtype=jnp.int32)
    residue = (lanes[:, None] * wave_line[None, :]) % points
    phase = residue.astype(jnp.float32) * (2.0 * math.pi / points.astype(jnp.float32))
    cosine = jnp.cos(phase)[:, None, :]
    sine_part = jnp.sin(phase)[:, None, :]
    weight = jnp.where(wave_line == 0, jnp.float32(1.0), jnp.float32(2.0)) * (2 * wave_line < points).astype(jnp.float32)
    real_part = coeffs[None, :, 0, :]
    imag_part = coeffs[None, :, 1, :]
    turned_re = weight * (real_part * cosine - imag_part * sine_part)
    turned_im = weight * (real_part * sine_part + imag_part * cosine)
    return jnp.concatenate([turned_re, turned_im], 2).astype(jnp.bfloat16)


def estimate_column(kelvin_by_stratum, moisture_by_stratum, bottom_boundary, elevation_array):
    kelvin_field = 288.0 + 12.0 * kelvin_by_stratum
    water_vapour_share = 0.008 + 0.002 * moisture_by_stratum
    density_weighted_kelvin = kelvin_field * (1.0 + 0.608 * water_vapour_share)
    stratum_average = jnp.concatenate([density_weighted_kelvin[:1], 0.5 * (density_weighted_kelvin[1:] + density_weighted_kelvin[:-1])], 0)
    heights_lev = jnp.cumsum(thickness_scale * stratum_average, axis=0)
    mixing_weight = jnp.clip((elevation_array[None] - heights_lev[:-1]) / (heights_lev[1:] - heights_lev[:-1]), 0.0, 1.0)
    kelvin_interpolated = kelvin_field[0] + jnp.sum(mixing_weight * (kelvin_field[1:] - kelvin_field[:-1]), 0)
    moisture_interpolated = water_vapour_share[0] + jnp.sum(mixing_weight * (water_vapour_share[1:] - water_vapour_share[:-1]), 0)
    logarithmic_barometric = math.log(1.0e5) + 0.15 * bottom_boundary - log_step * (1.0 + jnp.sum(mixing_weight, 0))
    vapour_maximum = 611.2 * jnp.exp(17.67 * (kelvin_interpolated - 273.15) / (kelvin_interpolated - 29.65))
    return (kelvin_interpolated - 288.0) / 12.0, moisture_interpolated * jnp.exp(logarithmic_barometric) / (0.622 * vapour_maximum)


def reference(spec_tq, spec_sp, legendre, low_wavenumber, lon_points, requested_elevation):
    position = jnp.arange(K, dtype=jnp.int32)
    spectra = jnp.concatenate([spec_tq.reshape(PAIRS, 4 * STRATUM_COUNT, K), spec_sp], 1)
    channels = 4 * STRATUM_COUNT + 2

    def one_pair(pair_args):
        plane, spectrum, low_one = pair_args
        boundary = MW - low_one
        higher = position >= boundary
        odd_degree = jnp.where(higher, position - boundary, position) % 2 == 1
        selectors = jnp.stack([~higher & ~odd_degree, ~higher & odd_degree, higher & ~odd_degree, higher & odd_degree], 0)
        selected = jnp.where(selectors[:, None, :], spectrum[None], jnp.zeros((), jnp.bfloat16)).reshape(4 * channels, K)
        return jnp.dot(plane, selected.T, preferred_element_type=jnp.float32).reshape(LATH, 4, channels)

    partial_sums = lax.map(one_pair, (legendre, spectra, low_wavenumber))
    northern = partial_sums[:, :, 0::2] + partial_sums[:, :, 1::2]
    southern = partial_sums[:, :, 0::2] - partial_sums[:, :, 1::2]
    merged = jnp.concatenate([northern, southern[:, ::-1]], 1)
    fourier = jnp.transpose(merged, (1, 3, 0, 2)).reshape(LAT, channels // 2, 2, MW)
    slot_index = jnp.arange(MW, dtype=jnp.int32)
    pair_low = low_wavenumber[slot_index // 2]
    wave_line = jnp.where(slot_index % 2 == 0, pair_low, MW - 1 - pair_low)
    all_rows = jnp.arange(LAT, dtype=jnp.int32)
    row_ids = jnp.where(all_rows < LATH, all_rows, LAT - 1 - all_rows)
    grid_point_rows = lon_points[row_ids]
    group_ids = jnp.arange(LONPAD // group_width, dtype=jnp.int32)

    def one_row(row_args):
        coeffs, points = row_args
        turned = twisted(coeffs, wave_line, points).astype(jnp.float32)
        table = wave_table(wave_line, points, group_ids).astype(jnp.float32)
        return jnp.einsum("qfj,jp->fpq", turned, table).reshape(channels // 2, LONPAD)

    physical_space_data = lax.map(one_row, (fourier, grid_point_rows))
    longitude = jnp.arange(LONPAD, dtype=jnp.int32)
    inside = longitude[None, :] < grid_point_rows[:, None]
    physical_space_data = jnp.where(inside[:, None, :], physical_space_data, jnp.float32(0.0))
    kelvin_by_stratum = jnp.transpose(physical_space_data[:, :STRATUM_COUNT], (1, 0, 2))
    moisture_by_stratum = jnp.transpose(physical_space_data[:, STRATUM_COUNT:2 * STRATUM_COUNT], (1, 0, 2))
    bottom_boundary = physical_space_data[:, 2 * STRATUM_COUNT]
    kelvin_result, mixing_ratio_result = estimate_column(kelvin_by_stratum, moisture_by_stratum, bottom_boundary, requested_elevation.astype(jnp.float32))
    kelvin_result = jnp.where(inside, kelvin_result, jnp.float32(0.0))
    mixing_ratio_result = jnp.where(inside, mixing_ratio_result, jnp.float32(0.0))
    return kelvin_result, mixing_ratio_result
```

```python
import functools
import math

import jax
import jax.numpy as jnp
from jax import lax
from jax.experimental import pallas as pl
from jax.experimental.pallas import tpu as pltpu
from jax.sharding import PartitionSpec as P

lanes = 128
depth = 256
channel_rows = 16
near, far = 3, 25
thickness_scale = 0.012 * 287.05 / 9.80665
log_step = 0.012


def tile_of(t, g, fld_count):
    return t * fld_count + (g if t % 2 == 0 else fld_count - 1 - g)


def turned_over(rows):
    high = rows.astype(jnp.bfloat16)
    low = (rows - high.astype(jnp.float32)).astype(jnp.bfloat16)
    row = lax.broadcasted_iota(jnp.int32, (lanes, 2 * lanes), 0)
    column = lax.broadcasted_iota(jnp.int32, (lanes, 2 * lanes), 1)
    unit = (row == (column & (lanes - 1))).astype(jnp.float32).astype(jnp.bfloat16)
    return lax.dot_general(
        unit, jnp.concatenate([high, low], 1), (((1,), (1,)), ((), ())),
        preferred_element_type=jnp.float32,
    )


def legendre_kernel(
    sizes, low_ref, spec_ref, sp_ref, plane_ref, elevation_ref, known_ref, *rest
):
    fld_count, wn_count, pair_dev, group, last, levels, halves, turns, head, starts, pitches = sizes
    out_count = len(pitches) + (1 if head else 0)
    (*out_refs, matrix, total, even_rows, odd_rows, stage) = rest[: out_count + 5]
    sp_rows = out_refs.pop() if head else rest[-1]
    first_block = 0 if head else 1
    out_of = [0 if head else n for n in range(turns // 2)]
    half, step = pl.program_id(0), pl.program_id(1)
    block = step + first_block
    own, own_wn = lax.axis_index("fld"), lax.axis_index("wn")
    packed = last + 1
    channels = 4 * levels
    main_rows = 4 * channel_rows
    dest = fld_count * wn_count
    tiles = lanes // wn_count
    share = pair_dev // fld_count
    position = lax.broadcasted_iota(jnp.int32, (channel_rows, packed), 1)
    alternate = (1 - 2 * (position & 1)).astype(jnp.float32).astype(jnp.bfloat16)

    def build(i):
        pair = block * group + i
        low = low_ref[own_wn * pair_dev + pair]
        low_odd = (low & 1).astype(jnp.float32)
        below = position < last - low
        first = jnp.where(below, 1.0 - low_odd, low_odd).astype(jnp.bfloat16)
        flip = (1.0 - 2.0 * low_odd).astype(jnp.bfloat16)
        values = spec_ref[i].reshape(channels, packed)
        if channels < channel_rows:
            filler = jnp.zeros((channel_rows - channels, packed), jnp.bfloat16)
            values = jnp.concatenate([values, filler], 0)

        def four(values, first, alternate):
            swung = values * alternate
            even, even_swung = values * first, swung * first
            return even, even_swung * flip, values - even, swung - even_swung

        for n, rows in enumerate(four(values, first, alternate)):
            matrix[i, n * channel_rows : (n + 1) * channel_rows, :packed] = rows

        @pl.when((pair >= own * share) & (pair < (own + 1) * share))
        def _():
            pressure = sp_ref[i].astype(jnp.float32)
            single = first[:1].astype(jnp.float32)
            sign = alternate[:1].astype(jnp.float32)
            even, swung = pressure * single, pressure * sign
            even_swung = swung * single
            rows = [even, even_swung * flip.astype(jnp.float32), pressure - even, swung - even_swung]
            matrix[i, main_rows:, :packed] = jnp.concatenate(rows * 2, 0).astype(jnp.bfloat16)

    @pl.loop(0, group // 2)
    def _(n):
        build(2 * n)
        build(2 * n + 1)

    chunks = last // depth
    pitch = group + 1

    def widen(begin, end, buffer):
        for k in range(begin, end):
            rows = plane_ref[k].astype(jnp.float32)
            for n in range(group // 8):
                at = n * depth * far + (k % depth) * far
                buffer[pl.ds(at, 8, stride=near), :] = rows[8 * n : 8 * n + 8]

    buffers = (even_rows, odd_rows)
    widen(0, depth, buffers[0])
    for chunk in range(chunks):
        source, target = buffers[chunk % 2], buffers[(chunk + 1) % 2]
        for i in range(group):
            at = (i // 8) * depth * far + (i % 8) * near
            plane = source[pl.ds(at, depth, stride=far), :].astype(jnp.bfloat16)
            part = jnp.dot(
                matrix[i, :, chunk * depth : (chunk + 1) * depth],
                plane,
                preferred_element_type=jnp.float32,
            )
            if chunk == 0:
                total[i] = part
            else:
                total[i] += part
            if chunk + 1 < chunks:
                begin = (chunk + 1) * depth
                widen(begin + depth * i // group, begin + depth * (i + 1) // group, target)

    tail = plane_ref[last].astype(jnp.float32)
    low_lanes = lax.broadcasted_iota(jnp.int32, (wn_count, lanes), 1) < lanes // 2
    for first in range(0, group, 4):
        four = []
        for j in range(first, first + 4):
            column = matrix[j, :, last : last + 1].astype(jnp.float32)
            summed = total[j] + column * tail[j : j + 1]
            four.append(summed[:main_rows])
            at = ((half if head else block) * group + j) * 8
            sp_rows[pl.ds(pl.multiple_of(at, 8), 8), :] = summed[main_rows : main_rows + 8]
        quad = turned_over(jnp.concatenate(four, 0))
        for i in (first, first + 2):
            turned = quad[:, (i - first) * lanes // 2 :][:, :lanes]
            here = [turned[b * wn_count : (b + 1) * wn_count] for b in range(tiles)]
            moved = [pltpu.roll(tile, lanes // 2, 1) for tile in here]
            for n in range(turns // 2):
                for g in range(fld_count):
                    if halves == 1:
                        b, c = tile_of(2 * n, g, fld_count), tile_of(2 * n + 1, g, fld_count)
                        both = (
                            jnp.where(low_lanes, here[b], moved[c]),
                            jnp.where(low_lanes, moved[b], here[c]),
                        )
                    else:
                        c = fld_count - 1 - g
                        both = (
                            jnp.where(half == 0, here[g], moved[c]),
                            jnp.where(half == 0, moved[g], here[c]),
                        )
                    for j in range(2):
                        at = g * wn_count * pitch + i + j
                        stage[n, pl.ds(at, wn_count, stride=pitch), :] = both[j]

    for n in range(turns // 2):
        out = out_refs[out_of[n]]
        for d in range(dest):
            rows = stage[n, d * pitch : d * pitch + group, :]
            at = d * pitches[out_of[n]] + starts[n] + step * group
            at = pl.ds(pl.multiple_of(at, 8), group)
            if halves > 1:
                lane = lax.broadcasted_iota(jnp.int32, (group, lanes), 1)
                rows = jnp.where((lane < lanes // 2) & (half == 1), out[at, :], rows)
            out[at, :] = rows

    if head:
        slabs = elevation_ref.shape[1] // lanes
        band_rows = elevation_ref.shape[0]
        band_tiles = band_rows // wn_count

        @pl.when((half == 0) & (step == 0))
        def _():
            north = own_wn < wn_count // 2
            band = jnp.where(north, own_wn, wn_count - 1 - own_wn)
            turn = band * band_tiles // fld_count
            for d in range(dest):
                g, e = d // wn_count, d % wn_count
                tile = jnp.where(turn % 2 == 0, g, fld_count - 1 - g)
                inside = jnp.clip(turn * fld_count + tile - band * band_tiles, 0, band_tiles - 1)
                row = inside * wn_count + e
                row = jnp.where(north, row, band_rows - 1 - row)
                heights = elevation_ref[pl.ds(row, 1), :].astype(jnp.float32)
                for n in range(slabs):
                    at = d * pitches[0] + turns // 2 * group + n
                    out_refs[0][at : at + 1, :] = heights[:, n * lanes : (n + 1) * lanes]

        return

    @pl.when(step == 0)
    def _():
        sp_rows[: group * 8, :] = known_ref[pl.ds(pl.multiple_of(half * group * 8, 8), group * 8), :]

    out, row_pitch, carried = out_refs[-1], pitches[-1], pair_dev - group

    @pl.when(block == pair_dev // group - 1)
    def _():
        spot = lax.broadcasted_iota(jnp.int32, (wn_count, lanes), 1) // 32
        for n in range(-(-share // 4)):
            rows = sp_rows[pl.ds(pl.multiple_of((own * share + 4 * n) * 8, 8), 32), :]
            turned = turned_over(jnp.concatenate([rows] * 4, 0))
            here = [turned[b * wn_count : (b + 1) * wn_count] for b in range(tiles)]
            for g in range(fld_count):
                at = pl.ds(g * wn_count * row_pitch + carried + n, wn_count, stride=row_pitch)
                if halves == 1:
                    value = here[tile_of(turns - 1, g, fld_count)]
                    for t in range(turns - 1):
                        value = jnp.where(spot == t, here[tile_of(t, g, fld_count)], value)
                else:
                    value = jnp.where(half == 0, here[g], here[fld_count - 1 - g])
                    value = jnp.where((spot == 0) & (half == 1), out[at, :], value)
                out[at, :] = value


def legendre_sums(
    spec_tq, spec_sp, legendre, low_wavenumber, elevation, fld_count, wn_count, group, known
):
    pair_dev, _, levels, _, packed = spec_tq.shape
    half_rows = legendre.shape[1]
    last = packed - 1
    head = known is None
    turns = half_rows // (wn_count * fld_count)
    halves = half_rows // lanes
    planes = jnp.transpose(legendre, (2, 0, 1))
    dest = fld_count * wn_count
    rows = 4 * channel_rows + 16
    width = -(-packed // lanes) * lanes
    if head:
        starts, first_block, blocks = [n * group for n in range(turns // 2)], 0, 1
        slabs = elevation.shape[1] // lanes
        pitches = [-(-(group * turns // 2 + slabs) // 8) * 8]
        known = jnp.zeros((8, lanes), jnp.float32)
    else:
        starts, first_block, blocks = [0] * (turns // 2), 1, pair_dev // group - 1
        extra = -(-(pair_dev // fld_count) // 4)
        pitches = [pair_dev - group] * (turns // 2)
        pitches[-1] += -(-extra // 8) * 8
    sizes = (
        fld_count, wn_count, pair_dev, group, last, levels, halves, turns, head, tuple(starts), tuple(pitches)
    )
    shapes = [(dest * pitch, lanes) for pitch in pitches]
    outs = shapes + ([(halves * group * 8, lanes)] if head else [])
    work = blocks * group * (rows * last * lanes * 2) * halves
    out = pl.pallas_call(
        functools.partial(legendre_kernel, sizes),
        grid_spec=pltpu.PrefetchScalarGridSpec(
            num_scalar_prefetch=1,
            grid=(halves, blocks),
            in_specs=[
                pl.BlockSpec(
                    (group, 2, levels, 2, packed), lambda h, b, *_: (b + first_block, 0, 0, 0, 0)
                ),
                pl.BlockSpec((group, 2, packed), lambda h, b, *_: (b + first_block, 0, 0)),
                pl.BlockSpec((packed, group, lanes), lambda h, b, *_: (0, b + first_block, h)),
                pl.BlockSpec(elevation.shape, lambda h, b, *_: (0, 0)),
                pl.BlockSpec(known.shape, lambda h, b, *_: (0, 0)),
            ],
            out_specs=[pl.BlockSpec(shape, lambda h, b, *_: (0, 0)) for shape in outs],
            scratch_shapes=[
                pltpu.VMEM((group, rows, width), jnp.bfloat16),
                pltpu.VMEM((group, rows, lanes), jnp.float32),
                pltpu.VMEM((group // 8 * depth * far, lanes), jnp.float32),
                pltpu.VMEM((group // 8 * depth * far, lanes), jnp.float32),
                pltpu.VMEM((turns // 2, dest * (group + 1), lanes), jnp.float32),
            ]
            + ([] if head else [pltpu.VMEM((pair_dev * 8 + 32, lanes), jnp.float32)]),
        ),
        out_shape=[jax.ShapeDtypeStruct(shape, jnp.float32) for shape in outs],
        compiler_params=pltpu.CompilerParams(vmem_limit_bytes=56 * 1024 * 1024),
        cost_estimate=pl.CostEstimate(
            flops=work, bytes_accessed=blocks * group * packed * lanes * 2 * halves, transcendentals=0
        ),
        name="legendre_head" if head else "legendre_rest",
    )(low_wavenumber, spec_tq, spec_sp, planes, elevation, known)
    return [block.reshape(dest, -1, lanes) for block in out[: len(pitches)]] + list(out[len(pitches) :])


def sine_cosine(numbers, points):
    ratio = 1.0 / points
    rest = numbers - jnp.round(numbers * ratio) * points
    x = rest * (math.pi * ratio)
    y = x * x
    sine = jnp.float32(-1.0 / 39916800.0)
    for factor in (1.0 / 362880.0, -1.0 / 5040.0, 1.0 / 120.0, -1.0 / 6.0, 1.0):
        sine = sine * y + jnp.float32(factor)
    sine = sine * x
    cosine = jnp.float32(1.0 / 479001600.0)
    for factor in (-1.0 / 3628800.0, 1.0 / 40320.0, -1.0 / 720.0, 1.0 / 24.0, -0.5, 1.0):
        cosine = cosine * y + jnp.float32(factor)
    return 1.0 - 2.0 * sine * sine, 2.0 * sine * cosine


def synthesis_kernel(
    sizes, points_ref, low_ref, head_ref, coeff_ref, pressure_ref, out_ref,
    turned_ref, angle_ref, left_ref, table_ref, first_ref, second_ref, height_ref, moved_ref,
):
    fld_count, wn_count, levels, wave_count, tall, units, slabs, band_tiles, first_turn, group, turn_pairs = sizes
    pairs = wave_count // 2
    pair_dev = pairs // wn_count
    rest = pair_dev - group
    head_rows = group * turn_pairs
    own, own_wn = lax.axis_index("fld"), lax.axis_index("wn")
    stratum_count = fld_count * levels
    fields = 2 * stratum_count + 1
    low = low_ref[...]
    low_even = low % 2 == 0
    mirror = wave_count - 1 - low
    waves = (jnp.where(low_even, low, mirror), jnp.where(low_even, mirror, low))

    for g in range(fld_count):
        blocks = []
        for d in range(g * wn_count, (g + 1) * wn_count):
            at = first_turn // 2 * group
            blocks += [head_ref[d, at : at + group, :], coeff_ref[d, :rest, :]]
        turned_ref[g] = turned_over(jnp.concatenate(blocks, 0))

    eight = lax.broadcasted_iota(jnp.int32, (8, 1), 0).astype(jnp.float32)
    lane = lax.broadcasted_iota(jnp.int32, (8, lanes), 1)
    spot = lax.broadcasted_iota(jnp.int32, (8, lanes), 0) * lanes + lane

    @pl.loop(0, 2)
    def _(t):
        tile = (first_turn + t) * fld_count + jnp.where(t == 0, own, fld_count - 1 - own)
        band = tile // band_tiles
        points = points_ref[tile * wn_count + own_wn]
        real_points = points.astype(jnp.float32)
        middle = points // 2
        unit_count = (middle + 1023) // 1024
        whole_rows = middle // lanes
        left_over = middle - whole_rows * lanes

        spin = []
        for parity in range(2):
            wave = waves[parity]
            number = wave.astype(jnp.float32)
            weight = jnp.where(wave == 0, 1.0, 2.0) * jnp.where(2 * wave < points, 1.0, 0.0)
            cosine, sine = sine_cosine(number * (eight * 128.0), real_points)
            spin.append((cosine * weight, sine * weight))
            base_cosine, base_sine = sine_cosine(number * eight, real_points)
            @pl.loop(0, unit_count)
            def _(u, parity=parity, base_cosine=base_cosine, base_sine=base_sine, number=number):
                for part in range(2):
                    steps = eight * 8.0 + (64.0 * part + 1024.0 * u.astype(jnp.float32))
                    turns = sine_cosine(number * steps, real_points)
                    for n in range(2):
                        angle_ref[parity, n, part * 8 : (part + 1) * 8, :] = turns[n]
                for step in range(0, 16, 2):
                    cosines, sines = [], []
                    for one in (step, step + 1):
                        turn_cosine = angle_ref[parity, 0, one : one + 1, :]
                        turn_sine = angle_ref[parity, 1, one : one + 1, :]
                        cosines.append(base_cosine * turn_cosine - base_sine * turn_sine)
                        sines.append(-(base_sine * turn_cosine + base_cosine * turn_sine))
                    at = pl.ds(pl.multiple_of(u * lanes + step * 8, 16), 16)
                    table_ref[parity, at, :pairs] = jnp.concatenate(cosines, 0).astype(jnp.bfloat16)
                    table_ref[parity, at, pairs:] = jnp.concatenate(sines, 0).astype(jnp.bfloat16)

        for side in range(2):
            for parity in range(2):
                cosine, sine = spin[parity]

                def twist(real, imag, cosine=cosine, sine=sine):
                    return real * cosine - imag * sine, real * sine + imag * cosine

                at = t * 4 * channel_rows + (parity * 2 + side) * channel_rows
                for field in range(0, fields, 2):
                    reals, imags = [], []
                    for one in (field, field + 1):
                        if one < fields - 1:
                            kind, stratum = one // stratum_count, one % stratum_count
                            row = at + (kind * levels + stratum % levels) * 2
                            real = turned_ref[stratum // levels, pl.ds(row, 1), :]
                            imag = turned_ref[stratum // levels, pl.ds(row + 1, 1), :]
                        elif one == fields - 1:
                            row = (parity * 2 + side) * 2
                            real = pressure_ref[t, pl.ds(row, 1), :]
                            imag = pressure_ref[t, pl.ds(row + 1, 1), :]
                        else:
                            reals.append(jnp.zeros((8, pairs), jnp.float32))
                            imags.append(jnp.zeros((8, pairs), jnp.float32))
                            continue
                        turned = twist(real, imag)
                        reals.append(turned[0])
                        imags.append(turned[1])
                    rows = slice(field * 8, (field + 2) * 8)
                    left_ref[side, parity, rows, :pairs] = jnp.concatenate(reals, 0).astype(jnp.bfloat16)
                    left_ref[side, parity, rows, pairs:] = jnp.concatenate(imags, 0).astype(jnp.bfloat16)

            source = band if side == 0 else wn_count - 1 - band
            for g in range(fld_count):
                height_ref[g * slabs : (g + 1) * slabs, :] = head_ref[
                    g * wn_count + source, head_rows : head_rows + slabs, :
                ]

            @pl.loop(0, unit_count)
            def _(u, side=side):
                sums = []
                for parity in range(2):
                    table = table_ref[parity, pl.ds(pl.multiple_of(u * lanes, lanes), lanes), :]
                    sums.append(
                        lax.dot_general(
                            left_ref[side, parity], table, (((1,), (1,)), ((), ())),
                            preferred_element_type=jnp.float32,
                        )
                    )
                first_ref[...] = sums[0] + sums[1]
                second_ref[...] = sums[0] - sums[1]
                begin = pl.multiple_of(u * 8, 8)
                for which, grid_ref in enumerate((first_ref, second_ref)):
                    if which == 0:
                        height = height_ref[pl.ds(begin, 8), :]
                    else:
                        back = lax.rem(lanes - left_over, lanes)
                        upper = pltpu.roll(height_ref[pl.ds(begin + whole_rows, 8), :], back, 1)
                        lower = pltpu.roll(height_ref[pl.ds(begin + whole_rows + 1, 8), :], back, 1)
                        height = jnp.where(lane < lanes - left_over, upper, lower)
                    warmth, moisture = estimate_column(grid_ref, height, stratum_count)
                    moved_ref[which, 0, pl.ds(32 + begin, 8), :] = warmth
                    moved_ref[which, 1, pl.ds(32 + begin, 8), :] = moisture

            for which in range(2):
                for tile in range(tall // 8):
                    place = spot + tile * 1024
                    near = moved_ref[0, which, 32 + tile * 8 : 40 + tile * 8, :] if tile < 3 else 0.0
                    start = 32 + tile * 8 - whole_rows
                    ahead = pltpu.roll(moved_ref[1, which, pl.ds(start, 8), :], left_over, 1)
                    behind = pltpu.roll(moved_ref[1, which, pl.ds(start - 1, 8), :], left_over, 1)
                    far = jnp.where(lane >= left_over, ahead, behind)
                    value = jnp.where(place < middle, near, far)
                    out_ref[t, side, which, tile * 8 : (tile + 1) * 8, :] = jnp.where(
                        place < points, value, 0.0
                    )


def estimate_column(grid_ref, height, stratum_count):
    def field(n):
        return grid_ref[n * 8 : (n + 1) * 8, :]

    kelvin = 288.0 + 12.0 * field(0)
    vapour = 0.008 + 0.002 * field(stratum_count)
    weighted = kelvin * (1.0 + 0.608 * vapour)
    level_height = thickness_scale * weighted
    kelvin_sum, vapour_sum, mixing_sum = kelvin, vapour, jnp.ones_like(kelvin)
    for k in range(1, stratum_count):
        next_kelvin = 288.0 + 12.0 * field(k)
        next_vapour = 0.008 + 0.002 * field(stratum_count + k)
        next_weighted = next_kelvin * (1.0 + 0.608 * next_vapour)
        thickness = (0.5 * thickness_scale) * (weighted + next_weighted)
        mixing = jnp.clip((height - level_height) / thickness, 0.0, 1.0)
        kelvin_sum = kelvin_sum + mixing * (next_kelvin - kelvin)
        vapour_sum = vapour_sum + mixing * (next_vapour - vapour)
        mixing_sum = mixing_sum + mixing
        level_height = level_height + thickness
        kelvin, vapour, weighted = next_kelvin, next_vapour, next_weighted
    log_pressure = math.log(100000.0) + 0.15 * field(2 * stratum_count) - log_step * mixing_sum
    exponent = 17.67 * (kelvin_sum - 273.15) / (kelvin_sum - 29.65)
    saturation = 611.2 * jnp.exp(exponent)
    return (
        (kelvin_sum - 288.0) * (1.0 / 12.0),
        vapour_sum * jnp.exp(log_pressure) / (0.622 * saturation),
    )


def synthesize(
    points, low_row, head, coeffs, pressure, levels, fld_count, slabs, band_tiles, first_turn, group, turn_pairs
):
    wn_count = coeffs.shape[0] // fld_count
    pairs = low_row.shape[1]
    wave_count = 2 * pairs
    tall = -(-fld_count * slabs // 8) * 8
    units = -(-fld_count * slabs * lanes // 2048)
    fields = 2 * fld_count * levels + 1
    rows = -(-fields // 2) * 16
    sizes = (fld_count, wn_count, levels, wave_count, tall, units, slabs, band_tiles, first_turn, group, turn_pairs)
    return pl.pallas_call(
        functools.partial(synthesis_kernel, sizes),
        in_specs=[pl.BlockSpec(memory_space=pltpu.SMEM)]
        + [pl.BlockSpec(memory_space=pltpu.VMEM)] * 4,
        out_specs=pl.BlockSpec(memory_space=pltpu.VMEM),
        out_shape=jax.ShapeDtypeStruct((2, 2, 2, tall, lanes), jnp.float32),
        scratch_shapes=[
            pltpu.VMEM((fld_count, lanes, pairs), jnp.float32),
            pltpu.VMEM((2, 2, 16, pairs), jnp.float32),
            pltpu.VMEM((2, 2, rows, wave_count), jnp.bfloat16),
            pltpu.VMEM((2, units * lanes, wave_count), jnp.bfloat16),
            pltpu.VMEM((rows, lanes), jnp.float32),
            pltpu.VMEM((rows, lanes), jnp.float32),
            pltpu.VMEM((tall + 32, lanes), jnp.float32),
            pltpu.VMEM((2, 2, 32 + tall + 32, lanes), jnp.float32),
        ],
        compiler_params=pltpu.CompilerParams(vmem_limit_bytes=48 * 1024 * 1024),
        cost_estimate=pl.CostEstimate(
            flops=8 * rows * wave_count * units * lanes, bytes_accessed=coeffs.size * 8, transcendentals=0
        ),
        name="synthesis",
    )(points, low_row, head, coeffs, pressure)


def shards(spec_tq, spec_sp, legendre, low_wavenumber, lon_points, requested_elevation):
    wn_count = lax.axis_size("wn")
    fld_count = lax.axis_size("fld")
    pair_dev, _, levels, _, packed = spec_tq.shape
    half_rows = legendre.shape[1]
    pairs = low_wavenumber.shape[0]
    band_rows, tile_width = requested_elevation.shape
    tile_count = half_rows // wn_count
    turns = tile_count // fld_count
    band_tiles = band_rows // wn_count
    wn_index = lax.axis_index("wn")
    fld_index = lax.axis_index("fld")
    everyone = ("fld", "wn")
    devices = fld_count * wn_count
    slabs = tile_width // lanes
    out_tall = slabs * fld_count

    group = 16 if pair_dev % 16 == 0 else 8

    def exchange(block):
        return lax.all_to_all(block, everyone, split_axis=0, concat_axis=0, tiled=True)

    arguments = (spec_tq, spec_sp, legendre, low_wavenumber, requested_elevation, fld_count, wn_count, group)
    first, known = legendre_sums(*arguments, None)
    head = exchange(first)
    sent = legendre_sums(*arguments, known)
    later, head = lax.optimization_barrier((sent[-1], head))
    carrier = exchange(later)
    arrived = [None] * (turns // 2)
    arrived[-1] = carrier
    for n in range(turns // 2 - 1):
        later, carrier = lax.optimization_barrier((sent[n], carrier))
        arrived[n] = exchange(later)

    share = pair_dev // fld_count
    share_rows = -(-share // 4)
    rest = pair_dev - group
    pressure = carrier[:, rest : rest + share_rows]
    pressure = pressure.reshape(fld_count, wn_count, share_rows, 4, 4, 8)[:, :, :, :turns]
    pressure = jnp.transpose(pressure, (3, 5, 1, 0, 2, 4))
    pressure = pressure.reshape(turns, 8, wn_count, fld_count, share_rows * 4)[..., :share]
    pressure = pressure.reshape(turns, 8, pairs)

    low_row = low_wavenumber.reshape(1, pairs)
    results = [None] * (turns // 2)
    for n in reversed(range(turns // 2)):
        results[n] = synthesize(
            lon_points, low_row, head, arrived[n], pressure[2 * n : 2 * n + 2], levels,
            fld_count, slabs, band_tiles, 2 * n, group, turns // 2,
        )

    north = wn_index < wn_count // 2
    band = jnp.where(north, wn_index, wn_count - 1 - wn_index)
    turn = band * band_tiles // fld_count
    own_row = jnp.arange(band_rows, dtype=jnp.int32)
    mirrored = jnp.where(north, own_row, band_rows - 1 - own_row)
    tile_in_turn = (band * band_tiles + mirrored // wn_count) % fld_count
    owner_for_row = (
        jnp.where(turn % 2 == 0, tile_in_turn, fld_count - 1 - tile_in_turn) * wn_count
        + mirrored % wn_count
    )
    result = jnp.concatenate(results, 0)[:, :, :, :out_tall]
    turn_of = [min(s, wn_count - 1 - s) * band_tiles // fld_count for s in range(wn_count)]
    side_of = [0 if s < wn_count // 2 else 1 for s in range(wn_count)]
    back = jnp.stack([result[t, side] for t, side in zip(turn_of, side_of)])
    back = back.reshape(wn_count, 2, fld_count, slabs, lanes)
    back = jnp.transpose(back, (2, 0, 1, 3, 4)).reshape(devices, 2, tile_width)
    back = lax.all_to_all(back, everyone, split_axis=0, concat_axis=0, tiled=True)
    back = jnp.take(back, owner_for_row, axis=0)
    return back[:, 0], back[:, 1]


def solution(mesh):
    in_specs = (
        P("wn", None, "fld", None, None),
        P("wn", None, None),
        P("wn", None, None),
        P(),
        P(),
        P("wn", "fld"),
    )
    out_specs = (P("wn", "fld"), P("wn", "fld"))
    return jax.shard_map(shards, mesh=mesh, in_specs=in_specs, out_specs=out_specs, check_vma=False)
```

```python
import functools
import math

import jax
import jax.numpy as jnp
from jax import lax
from jax.experimental import pallas as pl
from jax.experimental.pallas import tpu as pltpu
from jax.sharding import PartitionSpec as P

lanes = 128
depth = 256
channel_rows = 16
streams = 4
near, far = 3, 25
thickness_scale = 0.012 * 287.05 / 9.80665
log_step = 0.012


def tile_of(t, g, fld_count):
    return t * fld_count + (g if t % 2 == 0 else fld_count - 1 - g)


def turned_over(rows):
    high = rows.astype(jnp.bfloat16)
    low = (rows - high.astype(jnp.float32)).astype(jnp.bfloat16)
    row = lax.broadcasted_iota(jnp.int32, (lanes, 2 * lanes), 0)
    column = lax.broadcasted_iota(jnp.int32, (lanes, 2 * lanes), 1)
    unit = (row == (column & (lanes - 1))).astype(jnp.float32).astype(jnp.bfloat16)
    return lax.dot_general(
        unit, jnp.concatenate([high, low], 1), (((1,), (1,)), ((), ())),
        preferred_element_type=jnp.float32,
    )


def legendre_kernel(
    sizes, low_ref, spec_ref, sp_ref, *rest
):
    fld_count, wn_count, pair_dev, group, last, levels, halves, turns, head, starts, pitches = sizes
    plane_refs, tail_ref, extra_ref = rest[:streams], rest[streams], rest[streams + 1]
    rest = rest[streams + 2 :]
    out_count = len(pitches) + (1 if head else 0)
    (*out_refs, matrix, total, even_rows, odd_rows, stage) = rest[: out_count + 5]
    sp_rows = out_refs.pop() if head else rest[-1]
    first_block = 0 if head else 1
    out_of = [0 if head else n for n in range(turns // 2)]
    half, step = pl.program_id(0), 0 if head else pl.program_id(1)
    block = step + first_block
    own, own_wn = lax.axis_index("fld"), lax.axis_index("wn")
    packed = last + 1
    channels = 4 * levels
    main_rows = 4 * channel_rows
    dest = fld_count * wn_count
    tiles = lanes // wn_count
    share = pair_dev // fld_count
    position = lax.broadcasted_iota(jnp.int32, (channel_rows, packed), 1)
    alternate = (1 - 2 * (position & 1)).astype(jnp.float32).astype(jnp.bfloat16)

    def build(i):
        pair = block * group + i
        low = low_ref[own_wn * pair_dev + pair]
        low_odd = (low & 1).astype(jnp.float32)
        below = position < last - low
        first = jnp.where(below, 1.0 - low_odd, low_odd).astype(jnp.bfloat16)
        flip = (1.0 - 2.0 * low_odd).astype(jnp.bfloat16)
        values = spec_ref[i].reshape(channels, packed)
        if channels < channel_rows:
            filler = jnp.zeros((channel_rows - channels, packed), jnp.bfloat16)
            values = jnp.concatenate([values, filler], 0)

        def four(values, first, alternate):
            swung = values * alternate
            even, even_swung = values * first, swung * first
            return even, even_swung * flip, values - even, swung - even_swung

        for n, rows in enumerate(four(values, first, alternate)):
            matrix[i, n * channel_rows : (n + 1) * channel_rows, :packed] = rows

        @pl.when((pair >= own * share) & (pair < (own + 1) * share))
        def _():
            pressure = sp_ref[i].astype(jnp.float32)
            single = first[:1].astype(jnp.float32)
            sign = alternate[:1].astype(jnp.float32)
            even, swung = pressure * single, pressure * sign
            even_swung = swung * single
            rows = [even, even_swung * flip.astype(jnp.float32), pressure - even, swung - even_swung]
            matrix[i, main_rows:, :packed] = jnp.concatenate(rows * 2, 0).astype(jnp.bfloat16)

    def build_all():
        @pl.loop(0, group // 2)
        def _(n):
            build(2 * n)
            build(2 * n + 1)

    chunks = last // depth
    stream = last // streams
    pitch = group + 1

    def widen(begin, end, buffer):
        for k in range(begin, end):
            rows = plane_refs[k // stream][k % stream].astype(jnp.float32)
            for n in range(group // 8):
                at = n * depth * far + (k % depth) * far
                buffer[pl.ds(at, 8, stride=near), :] = rows[8 * n : 8 * n + 8]

    def plane_of(i, source):
        at = (i // 8) * depth * far + (i % 8) * near
        return source[pl.ds(at, depth, stride=far), :].astype(jnp.bfloat16)

    def sum_all():
        buffers = (even_rows, odd_rows)
        widen(0, depth, buffers[0])
        for chunk in range(chunks):
            source, target = buffers[chunk % 2], buffers[(chunk + 1) % 2]
            for i in range(group):
                plane = plane_of(i, source)
                part = jnp.dot(
                    matrix[i, :, chunk * depth : (chunk + 1) * depth],
                    plane,
                    preferred_element_type=jnp.float32,
                )
                if chunk == 0:
                    total[i] = part
                else:
                    total[i] += part
                if chunk + 1 < chunks:
                    begin = (chunk + 1) * depth
                    widen(begin + depth * i // group, begin + depth * (i + 1) // group, target)

    def finish():
        tail = tail_ref[0].astype(jnp.float32)
        low_lanes = lax.broadcasted_iota(jnp.int32, (wn_count, lanes), 1) < lanes // 2
        for first in range(0, group, 4):
            four = []
            for j in range(first, first + 4):
                column = matrix[j, :, last : last + 1].astype(jnp.float32)
                summed = total[j] + column * tail[j : j + 1]
                four.append(summed[:main_rows])
                at = ((half if head else block) * group + j) * 8
                sp_rows[pl.ds(pl.multiple_of(at, 8), 8), :] = summed[main_rows : main_rows + 8]
            quad = turned_over(jnp.concatenate(four, 0))
            for i in (first, first + 2):
                turned = quad[:, (i - first) * lanes // 2 :][:, :lanes]
                here = [turned[b * wn_count : (b + 1) * wn_count] for b in range(tiles)]
                moved = [pltpu.roll(tile, lanes // 2, 1) for tile in here]
                for n in range(turns // 2):
                    for g in range(fld_count):
                        if halves == 1:
                            b, c = tile_of(2 * n, g, fld_count), tile_of(2 * n + 1, g, fld_count)
                            both = (
                                jnp.where(low_lanes, here[b], moved[c]),
                                jnp.where(low_lanes, moved[b], here[c]),
                            )
                        else:
                            c = fld_count - 1 - g
                            both = (
                                jnp.where(half == 0, here[g], moved[c]),
                                jnp.where(half == 0, moved[g], here[c]),
                            )
                        for j in range(2):
                            at = g * wn_count * pitch + i + j
                            stage[n, pl.ds(at, wn_count, stride=pitch), :] = both[j]

        for n in range(turns // 2):
            out = out_refs[out_of[n]]
            for d in range(dest):
                rows = stage[n, d * pitch : d * pitch + group, :]
                at = d * pitches[out_of[n]] + starts[n] + step * group
                at = pl.ds(pl.multiple_of(at, 8), group)
                if halves > 1:
                    lane = lax.broadcasted_iota(jnp.int32, (group, lanes), 1)
                    rows = jnp.where((lane < lanes // 2) & (half == 1), out[at, :], rows)
                out[at, :] = rows

    build_all()
    sum_all()
    finish()

    if head:
        slabs = extra_ref.shape[1] // lanes
        band_rows = extra_ref.shape[0]
        band_tiles = band_rows // wn_count

        @pl.when(half == 0)
        def _():
            north = own_wn < wn_count // 2
            band = jnp.where(north, own_wn, wn_count - 1 - own_wn)
            turn = band * band_tiles // fld_count
            for d in range(dest):
                g, e = d // wn_count, d % wn_count
                tile = jnp.where(turn % 2 == 0, g, fld_count - 1 - g)
                inside = jnp.clip(turn * fld_count + tile - band * band_tiles, 0, band_tiles - 1)
                row = inside * wn_count + e
                row = jnp.where(north, row, band_rows - 1 - row)
                heights = extra_ref[pl.ds(row, 1), :].astype(jnp.float32)
                for n in range(slabs):
                    at = d * pitches[0] + turns // 2 * group + n
                    out_refs[0][at : at + 1, :] = heights[:, n * lanes : (n + 1) * lanes]

        return

    @pl.when(step == 0)
    def _():
        sp_rows[: group * 8, :] = extra_ref[pl.ds(pl.multiple_of(half * group * 8, 8), group * 8), :]

    out, row_pitch, carried = out_refs[-1], pitches[-1], pair_dev - group

    @pl.when(block == pair_dev // group - 1)
    def _():
        spot = lax.broadcasted_iota(jnp.int32, (wn_count, lanes), 1) // 32
        for n in range(-(-share // 4)):
            rows = sp_rows[pl.ds(pl.multiple_of((own * share + 4 * n) * 8, 8), 32), :]
            turned = turned_over(jnp.concatenate([rows] * 4, 0))
            here = [turned[b * wn_count : (b + 1) * wn_count] for b in range(tiles)]
            for g in range(fld_count):
                at = pl.ds(g * wn_count * row_pitch + carried + n, wn_count, stride=row_pitch)
                if halves == 1:
                    value = here[tile_of(turns - 1, g, fld_count)]
                    for t in range(turns - 1):
                        value = jnp.where(spot == t, here[tile_of(t, g, fld_count)], value)
                else:
                    value = jnp.where(half == 0, here[g], here[fld_count - 1 - g])
                    value = jnp.where((spot == 0) & (half == 1), out[at, :], value)
                out[at, :] = value


def legendre_sums(
    spec_tq, spec_sp, legendre, low_wavenumber, elevation, fld_count, wn_count, group, known
):
    pair_dev, _, levels, _, packed = spec_tq.shape
    half_rows = legendre.shape[1]
    last = packed - 1
    head = known is None
    turns = half_rows // (wn_count * fld_count)
    halves = half_rows // lanes
    planes = jnp.transpose(legendre, (2, 0, 1))
    dest = fld_count * wn_count
    rows = 4 * channel_rows + 16
    width = -(-packed // lanes) * lanes
    if head:
        starts, blocks = [n * group for n in range(turns // 2)], 1
        slabs = elevation.shape[1] // lanes
        pitches = [-(-(group * turns // 2 + slabs) // 8) * 8]
    else:
        starts, blocks = [0] * (turns // 2), pair_dev // group - 1
        share_rows = -(-(pair_dev // fld_count) // 4)
        pitches = [pair_dev - group] * (turns // 2)
        pitches[-1] += -(-share_rows // 8) * 8
    sizes = (
        fld_count, wn_count, pair_dev, group, last, levels, halves, turns, head, tuple(starts), tuple(pitches)
    )
    shapes = [(dest * pitch, lanes) for pitch in pitches]
    outs = shapes + ([(halves * group * 8, lanes)] if head else [])
    extra = elevation if head else known

    def pair_at(b):
        return 0 if head else b + 1

    plane_specs = [
        pl.BlockSpec((last // streams, group, lanes), lambda h, b, *_, n=n: (n, pair_at(b), h))
        for n in range(streams)
    ]
    work = blocks * group * (rows * last * lanes * 2) * halves
    out = pl.pallas_call(
        functools.partial(legendre_kernel, sizes),
        grid_spec=pltpu.PrefetchScalarGridSpec(
            num_scalar_prefetch=1,
            grid=(halves, blocks),
            in_specs=[
                pl.BlockSpec((group, 2, levels, 2, packed), lambda h, b, *_: (pair_at(b), 0, 0, 0, 0)),
                pl.BlockSpec((group, 2, packed), lambda h, b, *_: (pair_at(b), 0, 0)),
                *plane_specs,
                pl.BlockSpec((1, group, lanes), lambda h, b, *_: (last, pair_at(b), h)),
                pl.BlockSpec(extra.shape, lambda h, b, *_: (0, 0)),
            ],
            out_specs=[pl.BlockSpec(shape, lambda h, b, *_: (0, 0)) for shape in outs],
            scratch_shapes=[
                pltpu.VMEM((group, rows, width), jnp.bfloat16),
                pltpu.VMEM((group, rows, lanes), jnp.float32),
                pltpu.VMEM((group // 8 * depth * far, lanes), jnp.float32),
                pltpu.VMEM((group // 8 * depth * far, lanes), jnp.float32),
                pltpu.VMEM((turns // 2, dest * (group + 1), lanes), jnp.float32),
            ]
            + ([] if head else [pltpu.VMEM((pair_dev * 8 + 32, lanes), jnp.float32)]),
        ),
        out_shape=[jax.ShapeDtypeStruct(shape, jnp.float32) for shape in outs],
        compiler_params=pltpu.CompilerParams(vmem_limit_bytes=56 * 1024 * 1024),
        cost_estimate=pl.CostEstimate(
            flops=work, bytes_accessed=blocks * group * packed * lanes * 2 * halves, transcendentals=0
        ),
        name="legendre_head" if head else "legendre_rest",
    )(low_wavenumber, spec_tq, spec_sp, *[planes] * (streams + 1), extra)
    return [block.reshape(dest, -1, lanes) for block in out[: len(pitches)]] + list(out[len(pitches) :])


def sine_cosine(numbers, points):
    ratio = 1.0 / points
    rest = numbers - jnp.round(numbers * ratio) * points
    x = rest * (math.pi * ratio)
    y = x * x
    sine = jnp.float32(-1.0 / 39916800.0)
    for factor in (1.0 / 362880.0, -1.0 / 5040.0, 1.0 / 120.0, -1.0 / 6.0, 1.0):
        sine = sine * y + jnp.float32(factor)
    sine = sine * x
    cosine = jnp.float32(1.0 / 479001600.0)
    for factor in (-1.0 / 3628800.0, 1.0 / 40320.0, -1.0 / 720.0, 1.0 / 24.0, -0.5, 1.0):
        cosine = cosine * y + jnp.float32(factor)
    return 1.0 - 2.0 * sine * sine, 2.0 * sine * cosine


def synthesis_kernel(
    sizes, points_ref, low_ref, head_ref, coeff_ref, pressure_ref, out_ref,
    turned_ref, angle_ref, left_ref, table_ref, first_ref, second_ref, height_ref, moved_ref,
):
    fld_count, wn_count, levels, wave_count, tall, units, slabs, band_tiles, first_turn, group, turn_pairs = sizes
    pairs = wave_count // 2
    pair_dev = pairs // wn_count
    rest = pair_dev - group
    head_rows = group * turn_pairs
    own, own_wn = lax.axis_index("fld"), lax.axis_index("wn")
    stratum_count = fld_count * levels
    fields = 2 * stratum_count + 1
    low = low_ref[...]
    low_even = low % 2 == 0
    mirror = wave_count - 1 - low
    waves = (jnp.where(low_even, low, mirror), jnp.where(low_even, mirror, low))

    for g in range(fld_count):
        blocks = []
        for d in range(g * wn_count, (g + 1) * wn_count):
            at = first_turn // 2 * group
            blocks += [head_ref[d, at : at + group, :], coeff_ref[d, :rest, :]]
        turned_ref[g] = turned_over(jnp.concatenate(blocks, 0))

    eight = lax.broadcasted_iota(jnp.int32, (8, 1), 0).astype(jnp.float32)
    four = (lax.broadcasted_iota(jnp.int32, (8, 1), 0) & 3).astype(jnp.float32)
    northern = lax.broadcasted_iota(jnp.int32, (8, pairs), 0) < 4
    lane = lax.broadcasted_iota(jnp.int32, (8, lanes), 1)
    spot = lax.broadcasted_iota(jnp.int32, (8, lanes), 0) * lanes + lane

    @pl.loop(0, 2)
    def _(t):
        tile = (first_turn + t) * fld_count + jnp.where(t == 0, own, fld_count - 1 - own)
        band = tile // band_tiles
        points = points_ref[tile * wn_count + own_wn]
        real_points = points.astype(jnp.float32)
        middle = points // 2
        unit_count = (middle + 1023) // 1024
        whole_rows = middle // lanes
        left_over = middle - whole_rows * lanes

        for side in range(2):
            source = band if side == 0 else wn_count - 1 - band
            for g in range(fld_count):
                height_ref[side, g * slabs : (g + 1) * slabs, :] = head_ref[
                    g * wn_count + source, head_rows : head_rows + slabs, :
                ]

        for parity in range(2):
            wave = waves[parity]
            number = wave.astype(jnp.float32)
            weight = jnp.where(wave == 0, 1.0, 2.0) * jnp.where(2 * wave < points, 1.0, 0.0)
            cosine, sine = sine_cosine(number * (four * 256.0), real_points)
            cosine, sine = cosine * weight, sine * weight
            base_cosine, base_sine = sine_cosine(number * eight, real_points)

            at = t * 4 * channel_rows + parity * 2 * channel_rows
            for field in range(0, fields, 2):
                reals, imags = [], []
                for one in (field, field + 1):
                    if one == fields:
                        reals.append(jnp.zeros((8, pairs), jnp.float32))
                        imags.append(jnp.zeros((8, pairs), jnp.float32))
                        continue
                    parts = []
                    for imag in range(2):
                        if one < fields - 1:
                            kind, stratum = one // stratum_count, one % stratum_count
                            row = at + (kind * levels + stratum % levels) * 2 + imag
                            north = turned_ref[stratum // levels, pl.ds(row, 1), :]
                            south = turned_ref[stratum // levels, pl.ds(row + channel_rows, 1), :]
                        else:
                            row = parity * 4 + imag
                            north = pressure_ref[t, row : row + 1, :]
                            south = pressure_ref[t, row + 2 : row + 3, :]
                        parts.append(jnp.where(northern, north, south))
                    reals.append(parts[0] * cosine - parts[1] * sine)
                    imags.append(parts[0] * sine + parts[1] * cosine)
                rows = slice(field * 8, (field + 2) * 8)
                left_ref[parity, rows, :pairs] = jnp.concatenate(reals, 0).astype(jnp.bfloat16)
                left_ref[parity, rows, pairs:] = jnp.concatenate(imags, 0).astype(jnp.bfloat16)

            @pl.loop(0, unit_count)
            def _(u, parity=parity, base_cosine=base_cosine, base_sine=base_sine, number=number):
                for part in range(4):
                    steps = eight * 8.0 + (64.0 * part + 1024.0 * u.astype(jnp.float32))
                    turns = sine_cosine(number * steps, real_points)
                    for n in range(2):
                        angle_ref[parity, n, part * 8 : (part + 1) * 8, :] = turns[n]
                for step in range(0, 32, 2):
                    cosines, sines = [], []
                    for one in (step, step + 1):
                        turn_cosine = angle_ref[parity, 0, one : one + 1, :]
                        turn_sine = angle_ref[parity, 1, one : one + 1, :]
                        cosines.append(base_cosine * turn_cosine - base_sine * turn_sine)
                        sines.append(-(base_sine * turn_cosine + base_cosine * turn_sine))
                    at = pl.ds(pl.multiple_of(u * 2 * lanes + step * 8, 16), 16)
                    table_ref[parity, at, :pairs] = jnp.concatenate(cosines, 0).astype(jnp.bfloat16)
                    table_ref[parity, at, pairs:] = jnp.concatenate(sines, 0).astype(jnp.bfloat16)

        @pl.loop(0, unit_count)
        def _(u):
            sums = []
            for parity in range(2):
                at = pl.ds(pl.multiple_of(u * 2 * lanes, lanes), 2 * lanes)
                sums.append(
                    lax.dot_general(
                        left_ref[parity], table_ref[parity, at, :], (((1,), (1,)), ((), ())),
                        preferred_element_type=jnp.float32,
                    )
                )
            first_ref[...] = sums[0] + sums[1]
            second_ref[...] = sums[0] - sums[1]
            for column in range(2):
                begin = u * 8 + column

                def heights(start):
                    sides = [height_ref[side, pl.ds(start, 4, stride=2), :] for side in range(2)]
                    return jnp.concatenate(sides, 0)

                for which, grid_ref in enumerate((first_ref, second_ref)):
                    if which == 0:
                        height = heights(begin)
                    else:
                        back = lax.rem(lanes - left_over, lanes)
                        upper = pltpu.roll(heights(begin + whole_rows), back, 1)
                        lower = pltpu.roll(heights(begin + whole_rows + 1), back, 1)
                        height = jnp.where(lane < lanes - left_over, upper, lower)
                    columns = slice(column * lanes, (column + 1) * lanes)
                    results = estimate_column(grid_ref, columns, height, stratum_count)
                    for n, value in enumerate(results):
                        for side in range(2):
                            at = pl.ds(32 + begin, 4, stride=2)
                            moved_ref[which, n, side, at, :] = value[side * 4 : side * 4 + 4]

        for side in range(2):
            for which in range(2):
                for tile_row in range(tall // 8):
                    place = spot + tile_row * 1024
                    begin = 32 + tile_row * 8
                    near = moved_ref[0, which, side, begin : begin + 8, :] if tile_row < units else 0.0
                    start = begin - whole_rows
                    ahead = pltpu.roll(moved_ref[1, which, side, pl.ds(start, 8), :], left_over, 1)
                    behind = pltpu.roll(moved_ref[1, which, side, pl.ds(start - 1, 8), :], left_over, 1)
                    far = jnp.where(lane >= left_over, ahead, behind)
                    value = jnp.where(place < middle, near, far)
                    out_ref[t, side, which, tile_row * 8 : (tile_row + 1) * 8, :] = jnp.where(
                        place < points, value, 0.0
                    )


def estimate_column(grid_ref, columns, height, stratum_count):
    def field(n):
        return grid_ref[n * 8 : (n + 1) * 8, columns]

    kelvin = 288.0 + 12.0 * field(0)
    vapour = 0.008 + 0.002 * field(stratum_count)
    weighted = kelvin * (1.0 + 0.608 * vapour)
    level_height = thickness_scale * weighted
    kelvin_sum, vapour_sum, mixing_sum = kelvin, vapour, jnp.ones_like(kelvin)
    for k in range(1, stratum_count):
        next_kelvin = 288.0 + 12.0 * field(k)
        next_vapour = 0.008 + 0.002 * field(stratum_count + k)
        next_weighted = next_kelvin * (1.0 + 0.608 * next_vapour)
        thickness = (0.5 * thickness_scale) * (weighted + next_weighted)
        mixing = jnp.clip((height - level_height) / thickness, 0.0, 1.0)
        kelvin_sum = kelvin_sum + mixing * (next_kelvin - kelvin)
        vapour_sum = vapour_sum + mixing * (next_vapour - vapour)
        mixing_sum = mixing_sum + mixing
        level_height = level_height + thickness
        kelvin, vapour, weighted = next_kelvin, next_vapour, next_weighted
    log_pressure = math.log(100000.0) + 0.15 * field(2 * stratum_count) - log_step * mixing_sum
    exponent = 17.67 * (kelvin_sum - 273.15) / (kelvin_sum - 29.65)
    saturation = 611.2 * jnp.exp(exponent)
    return (
        (kelvin_sum - 288.0) * (1.0 / 12.0),
        vapour_sum * jnp.exp(log_pressure) / (0.622 * saturation),
    )


def synthesize(
    points, low_row, head, coeffs, pressure, levels, fld_count, slabs, band_tiles, first_turn, group, turn_pairs
):
    wn_count = coeffs.shape[0] // fld_count
    pairs = low_row.shape[1]
    wave_count = 2 * pairs
    tall = -(-fld_count * slabs // 8) * 8
    units = -(-fld_count * slabs * lanes // 2048)
    fields = 2 * fld_count * levels + 1
    rows = -(-fields // 2) * 16
    sizes = (fld_count, wn_count, levels, wave_count, tall, units, slabs, band_tiles, first_turn, group, turn_pairs)
    return pl.pallas_call(
        functools.partial(synthesis_kernel, sizes),
        in_specs=[pl.BlockSpec(memory_space=pltpu.SMEM)]
        + [pl.BlockSpec(memory_space=pltpu.VMEM)] * 4,
        out_specs=pl.BlockSpec(memory_space=pltpu.VMEM),
        out_shape=jax.ShapeDtypeStruct((2, 2, 2, tall, lanes), jnp.float32),
        scratch_shapes=[
            pltpu.VMEM((fld_count, lanes, pairs), jnp.float32),
            pltpu.VMEM((2, 2, 32, pairs), jnp.float32),
            pltpu.VMEM((2, rows, wave_count), jnp.bfloat16),
            pltpu.VMEM((2, units * 2 * lanes, wave_count), jnp.bfloat16),
            pltpu.VMEM((rows, 2 * lanes), jnp.float32),
            pltpu.VMEM((rows, 2 * lanes), jnp.float32),
            pltpu.VMEM((2, tall + 32, lanes), jnp.float32),
            pltpu.VMEM((2, 2, 2, 32 + tall + 32, lanes), jnp.float32),
        ],
        compiler_params=pltpu.CompilerParams(vmem_limit_bytes=48 * 1024 * 1024),
        cost_estimate=pl.CostEstimate(
            flops=8 * rows * wave_count * units * lanes, bytes_accessed=coeffs.size * 8, transcendentals=0
        ),
        name="synthesis",
    )(points, low_row, head, coeffs, pressure)


def shards(spec_tq, spec_sp, legendre, low_wavenumber, lon_points, requested_elevation):
    wn_count = lax.axis_size("wn")
    fld_count = lax.axis_size("fld")
    pair_dev, _, levels, _, packed = spec_tq.shape
    half_rows = legendre.shape[1]
    pairs = low_wavenumber.shape[0]
    band_rows, tile_width = requested_elevation.shape
    tile_count = half_rows // wn_count
    turns = tile_count // fld_count
    band_tiles = band_rows // wn_count
    wn_index = lax.axis_index("wn")
    fld_index = lax.axis_index("fld")
    everyone = ("fld", "wn")
    devices = fld_count * wn_count
    slabs = tile_width // lanes
    out_tall = slabs * fld_count

    group = 16 if pair_dev % 16 == 0 else 8

    def exchange(block):
        return lax.all_to_all(block, everyone, split_axis=0, concat_axis=0, tiled=True)

    arguments = (spec_tq, spec_sp, legendre, low_wavenumber, requested_elevation, fld_count, wn_count, group)
    first, known = legendre_sums(*arguments, None)
    head = exchange(first)
    sent = legendre_sums(*arguments, known)
    later, head = lax.optimization_barrier((sent[-1], head))
    carrier = exchange(later)
    arrived = [None] * (turns // 2)
    arrived[-1] = carrier
    for n in range(turns // 2 - 1):
        later, carrier = lax.optimization_barrier((sent[n], carrier))
        arrived[n] = exchange(later)

    share = pair_dev // fld_count
    share_rows = -(-share // 4)
    rest = pair_dev - group
    pressure = carrier[:, rest : rest + share_rows]
    pressure = pressure.reshape(fld_count, wn_count, share_rows, 4, 4, 8)[:, :, :, :turns]
    pressure = jnp.transpose(pressure, (3, 5, 1, 0, 2, 4))
    pressure = pressure.reshape(turns, 8, wn_count, fld_count, share_rows * 4)[..., :share]
    pressure = pressure.reshape(turns, 8, pairs)

    low_row = low_wavenumber.reshape(1, pairs)
    results = [None] * (turns // 2)
    for n in reversed(range(turns // 2)):
        results[n] = synthesize(
            lon_points, low_row, head, arrived[n], pressure[2 * n : 2 * n + 2], levels,
            fld_count, slabs, band_tiles, 2 * n, group, turns // 2,
        )

    north = wn_index < wn_count // 2
    band = jnp.where(north, wn_index, wn_count - 1 - wn_index)
    turn = band * band_tiles // fld_count
    own_row = jnp.arange(band_rows, dtype=jnp.int32)
    mirrored = jnp.where(north, own_row, band_rows - 1 - own_row)
    tile_in_turn = (band * band_tiles + mirrored // wn_count) % fld_count
    owner_for_row = (
        jnp.where(turn % 2 == 0, tile_in_turn, fld_count - 1 - tile_in_turn) * wn_count
        + mirrored % wn_count
    )
    result = jnp.concatenate(results, 0)[:, :, :, :out_tall]
    turn_of = [min(s, wn_count - 1 - s) * band_tiles // fld_count for s in range(wn_count)]
    side_of = [0 if s < wn_count // 2 else 1 for s in range(wn_count)]
    back = jnp.stack([result[t, side] for t, side in zip(turn_of, side_of)])
    back = back.reshape(wn_count, 2, fld_count, slabs, lanes)
    back = jnp.transpose(back, (2, 0, 1, 3, 4)).reshape(devices, 2, tile_width)
    back = lax.all_to_all(back, everyone, split_axis=0, concat_axis=0, tiled=True)
    back = jnp.take(back, owner_for_row, axis=0)
    return back[:, 0], back[:, 1]


def solution(mesh):
    in_specs = (
        P("wn", None, "fld", None, None),
        P("wn", None, None),
        P("wn", None, None),
        P(),
        P(),
        P("wn", "fld"),
    )
    out_specs = (P("wn", "fld"), P("wn", "fld"))
    return jax.shard_map(shards, mesh=mesh, in_specs=in_specs, out_specs=out_specs, check_vma=False)
```
